128 devices in a mesh: row: 32 (over x, z, y_hi), col: 4 (over y_lo, core).
Axes of the slice: x: 4, y: 4 (y_hi: 2, y_lo: 2; y = y_hi * 2 + y_lo), z: 4, core: 2. Of those that a mesh axis runs over, the one named last changes fastest.
Arguments:
- embeds: bfloat16 [1024, 256, 256], P(('row', 'col')), may hold values from -1.5 to 1.5
- panel_weight: bfloat16 [65536, 8192], P('row', 'col'), may hold values from -0.0234375 to 0.0234375
- cotangent: bfloat16 [1024, 8192], P('row', 'col'), may hold values from -6 to 6
Outputs:
- weight_grad: bfloat16 [65536, 8192], P('row', 'col')
- embed_grad: bfloat16 [1024, 256, 256], P(('row', 'col'))
The draws below stay inside these ranges and needn't reach their ends.
All inputs are finite; a program needn't handle non-finite values.
Results may differ from the reference program's by a relative error of at most 0.015.
Values may be sent and summed in bfloat16 or wider, within the bound.
No kernel may reach another device: no remote copies, remote signals or barrier semaphores. Data moves between devices by JAX's collectives and lax.ppermute only.
A program may use at most 128 MiB of HBM per device.

```python
import jax
import jax.numpy as jnp

FIELDS = 256
EMB_DIM = 256
PANEL = 8192
SAMPLES = 1024
FLAT = 65536
N_COL = 4


def steps_of(key, dims, cuts, low, largest):
    def one(position, shards_of):
        draws = jax.random.uniform(jax.random.fold_in(jax.random.fold_in(key, 6), position), (shards_of,), jnp.float32, low / len(cuts), largest / len(cuts))
        return jnp.repeat(jnp.exp(draws), dims[position] // shards_of).reshape((-1,) + (1,) * (len(dims) - position - 1))

    loudness = one(*cuts[0])
    for cut in cuts[1:]:
        loudness = loudness * one(*cut)
    return loudness


def centred(key, dims, scale, limit, cuts=(), held_as=jnp.bfloat16):
    drawn = jax.random.normal(key, dims, jnp.float32) * scale
    if len(cuts) > 0:
        drawn = steps_of(key, dims, cuts, -0.22, 0.18) * drawn
    return jnp.clip(drawn, min=-limit, max=limit).astype(held_as)


def setup_inputs(seed: int = 0) -> dict:
    key_of = jax.random.split(jax.random.key(seed), 4)
    return {
        "embeds": centred(key_of[0], (SAMPLES, FIELDS, EMB_DIM), 0.25, 1.5, ((0, 128),)),
        "panel_weight": centred(key_of[1], (FLAT, PANEL), FLAT ** -0.5, 0.0234375, ((0, 32), (1, 4))),
        "cotangent": centred(key_of[2], (SAMPLES, PANEL), 1.0, 6.0, ((0, 32), (1, 4))),
    }


def reference(embeds, panel_weight, cotangent):
    wide = embeds.astype(jnp.float32)
    gram = jnp.einsum('sid,sjd->sij', wide, wide).astype(jnp.bfloat16)
    gram_flat = gram.reshape(SAMPLES, FIELDS * FIELDS)
    weight_grad = jnp.dot(gram_flat.T, cotangent, preferred_element_type=jnp.float32).astype(jnp.bfloat16)
    group_width = PANEL // N_COL
    total = jnp.zeros((SAMPLES, FIELDS * FIELDS), jnp.float32)
    for group in range(N_COL):
        lower = group * group_width
        piece = jnp.dot(cotangent[:, lower:lower + group_width], panel_weight[:, lower:lower + group_width].T, preferred_element_type=jnp.float32)
        total = total + piece.astype(jnp.bfloat16).astype(jnp.float32)
    grad_gram = total.astype(jnp.bfloat16).reshape(SAMPLES, FIELDS, FIELDS).astype(jnp.float32)
    embed_grad = jnp.einsum('sij,sjd->sid', grad_gram, wide) + jnp.einsum('sji,sjd->sid', grad_gram, wide)
    return weight_grad, embed_grad.astype(jnp.bfloat16)
```

```python
import functools

import jax
import jax.numpy as jnp
from jax import lax
from jax.experimental import pallas as pl
from jax.experimental.pallas import tpu as pltpu
from jax.sharding import PartitionSpec as P

AXES = ("row", "col")
GRID = (4, 4, 2, 2, 2)
STEPS = ("xa", "za", "xb", "zb")
MASK = {"a": 1, "b": 3}
BF16 = jnp.bfloat16
F32 = jnp.float32


def pairs(x=0, z=0, yh=0, yl=0, core=0):
    out = []
    for device in range(128):
        c, l, h = device & 1, (device >> 1) & 1, (device >> 2) & 1
        zz, xx = (device >> 3) & 3, (device >> 5) & 3
        other = ((((xx ^ x) * 4 + (zz ^ z)) * 2 + (h ^ yh)) * 2 + (l ^ yl)) * 2 + (c ^ core)
        out.append((device, other))
    return out


def swap(value, **flips):
    return lax.ppermute(value, AXES, pairs(**flips))


def step_swap(value, step):
    return swap(value, **{step[0]: MASK[step[1]]})


def rotated(k):
    return STEPS[k:] + STEPS[:k]


def assemble_kernel(orders, place, *refs):
    out = refs[-1]
    x, z = place[0], place[1]
    for stream, order in enumerate(orders):
        halves = refs[2 * stream : 2 * stream + 2]
        for j in range(16):
            mx = mz = 0
            for t, step in enumerate(order):
                if (j >> t) & 1:
                    if step[0] == "x":
                        mx ^= MASK[step[1]]
                    else:
                        mz ^= MASK[step[1]]
            to = (x ^ mx) * 4 + (z ^ mz)
            start = pl.multiple_of(stream * 256 + to * 16, 16)
            out[pl.ds(start, 16), :] = halves[j // 8][(j % 8) * 16 : (j % 8) * 16 + 16, :]


def assemble(place, halves, orders):
    n = len(orders)
    return pl.pallas_call(
        functools.partial(assemble_kernel, orders),
        out_shape=jax.ShapeDtypeStruct((256 * n, 2048), BF16),
        in_specs=[pl.BlockSpec(memory_space=pltpu.SMEM)]
        + [pl.BlockSpec(memory_space=pltpu.VMEM)] * (2 * n),
        out_specs=pl.BlockSpec(memory_space=pltpu.VMEM),
        compiler_params=pltpu.CompilerParams(vmem_limit_bytes=24 << 20),
        cost_estimate=pl.CostEstimate(flops=0, bytes_accessed=n << 21, transcendentals=0),
    )(place, *halves)


def gather_stream(value, order):
    for step in order[:3]:
        value = jnp.concatenate([value, step_swap(value, step)], 0)
    return [value, step_swap(value, order[3])]


def weight_kernel(g0, g1, g2, g3, c0, c1, c2, c3, out):
    total = None
    for g, c in ((g0, c0), (g1, c1), (g2, c2), (g3, c3)):
        term = lax.dot_general(
            g[...], c[...], (((0,), (0,)), ((), ())), preferred_element_type=F32
        )
        total = term if total is None else total + term
    out[...] = total.astype(BF16)


def weight_product(grams, cots, tile=256):
    return pl.pallas_call(
        weight_kernel,
        grid=(2048 // tile,),
        out_shape=jax.ShapeDtypeStruct((2048, 2048), BF16),
        in_specs=[pl.BlockSpec((256, tile), lambda i: (0, i))] * 4
        + [pl.BlockSpec((256, 2048), lambda i, k=k: (k, 0)) for k in (0, 1, 0, 1)],
        out_specs=pl.BlockSpec((tile, 2048), lambda i: (i, 0)),
        compiler_params=pltpu.CompilerParams(vmem_limit_bytes=40 << 20),
        cost_estimate=pl.CostEstimate(
            flops=2 * 1024 * 2048 * 2048, bytes_accessed=16 << 20, transcendentals=0
        ),
    )(*grams, cots[0], cots[0], cots[1], cots[1])


def partial_product(cot, weight):
    return lax.dot_general(
        cot, weight, (((1,), (1,)), ((), ())), preferred_element_type=F32
    ).astype(BF16)


def add(*terms):
    total = terms[0].astype(F32)
    for term in terms[1:]:
        total = total + term.astype(F32)
    return total.astype(BF16)


def body(embeds, panel_weight, cotangent):
    local_count, field_count, width = embeds.shape
    row, col = lax.axis_index("row"), lax.axis_index("col")
    x, z, yh = row // 8, (row // 2) % 4, row % 2
    place = jnp.stack([x, z]).astype(jnp.int32)

    other = swap(cotangent, yh=1)
    low = jnp.where(yh == 0, cotangent, other).reshape(4, 8, 2048)
    high = jnp.where(yh == 0, other, cotangent).reshape(4, 8, 2048)
    both = jnp.stack([low, high], 1).reshape(4, 16, 2048)
    groups = [
        lax.dynamic_index_in_dim(both, col ^ k, 0, keepdims=False) for k in range(4)
    ]
    orders = [rotated(k) for k in (2, 3, 0, 1)]
    far_halves = gather_stream(groups[2], orders[2]) + gather_stream(groups[3], orders[3])
    near_halves = gather_stream(groups[0], orders[0]) + gather_stream(groups[1], orders[1])
    far = assemble(place, far_halves, orders[2:])
    near = assemble(place, near_halves, orders[:2])

    gram = jnp.einsum("sid,sjd->sij", embeds, embeds, preferred_element_type=F32)
    gram = gram.astype(BF16).reshape(local_count, field_count * field_count)

    far_sent = partial_product(far[256:], panel_weight)
    far_kept = partial_product(far[:256], panel_weight)
    far_sum = add(far_kept, swap(far_sent, core=1))
    gram, far_sum = lax.optimization_barrier((gram, far_sum))
    far_got = swap(far_sum, yl=1)
    near_sent = partial_product(near[256:], panel_weight)
    near_kept = partial_product(near[:256], panel_weight)
    near_got = swap(near_sent, core=1)

    gram_own = lax.all_to_all(gram, "row", split_axis=1, concat_axis=0, tiled=True)
    summed = add(near_kept, near_got, far_got)
    gram_far = swap(gram_own, yl=1)
    grad_gram = lax.all_to_all(summed, "row", split_axis=0, concat_axis=1, tiled=True)
    gram_core = swap(gram_own, core=1)
    gram_far_core = swap(gram_far, core=1)
    weight_grad = weight_product((gram_own, gram_core, gram_far, gram_far_core), (near, far))

    grad_gram = grad_gram.reshape(local_count, field_count, field_count)
    embed_grad = jnp.einsum("sij,sjd->sid", grad_gram, embeds, preferred_element_type=F32)
    embed_grad = embed_grad + jnp.einsum(
        "sji,sjd->sid", grad_gram, embeds, preferred_element_type=F32
    )
    return weight_grad, embed_grad.astype(BF16)


def solution(mesh):
    placed = (P(("row", "col"), None, None), P("row", "col"), P("row", "col"))
    return jax.shard_map(
        body,
        mesh=mesh,
        in_specs=placed,
        out_specs=(P("row", "col"), P(("row", "col"), None, None)),
        check_vma=False,
    )
```

```python
import functools

import jax
import jax.numpy as jnp
from jax import lax
from jax.experimental import pallas as pl
from jax.experimental.pallas import tpu as pltpu
from jax.sharding import PartitionSpec as P

AXES = ("row", "col")
MASK = {"a": 1, "b": 3}
BF16 = jnp.bfloat16
F32 = jnp.float32
TINY = pl.CostEstimate(flops=1000, bytes_accessed=1000, transcendentals=0)
FAR = (("xa", "za", "xb", "zb"), ("za", "xa", "zb", "xb"))
FAR_OTHER = FAR[::-1]
NEAR = (("xb", "zb", "xa", "za"), ("zb", "xb", "za", "xa"))
NEAR_OTHER = NEAR[::-1]


def pairs(flips):
    out = []
    for device in range(128):
        place = {
            "core": device & 1,
            "yl": (device >> 1) & 1,
            "yh": (device >> 2) & 1,
            "z": (device >> 3) & 3,
            "x": (device >> 5) & 3,
        }
        for axis, mask in flips[device & 1].items():
            place[axis] ^= mask
        other = (place["x"] * 4 + place["z"]) * 2 + place["yh"]
        out.append((device, (other * 2 + place["yl"]) * 2 + place["core"]))
    return out


def swap(value, **flips):
    return lax.ppermute(value, AXES, pairs((flips, flips)))


def step_swap(value, orders, t):
    flips = [{order[t][0]: MASK[order[t][1]]} for order in orders]
    return lax.ppermute(value, AXES, pairs(flips))


def doubled(value, orders, steps):
    for t in steps:
        value = jnp.concatenate([value, step_swap(value, orders, t)], -2)
    return value


def masks(order, j):
    mx = mz = 0
    for t, step in enumerate(order):
        if (j >> t) & 1:
            if step[0] == "x":
                mx ^= MASK[step[1]]
            else:
                mz ^= MASK[step[1]]
    return mx, mz


def block_of(place, orders, j):
    x, z, core = place[0], place[1], place[2]
    first, second = masks(orders[0], j), masks(orders[1], j)
    if first == second:
        return (x ^ first[0]) * 4 + (z ^ first[1])
    mx = jnp.where(core == 0, first[0], second[0])
    mz = jnp.where(core == 0, first[1], second[1])
    return (x ^ mx) * 4 + (z ^ mz)


def combine_kernel(place, own, got, far0, far1, out):
    for j in range(16):
        start = pl.multiple_of(block_of(place, NEAR, j) * 16, 16)
        out[pl.ds(start, 16), :] = own[j * 16 : j * 16 + 16, :]
    for orders, parts in ((NEAR_OTHER, (got,)), (FAR, (far0, far1))):
        for j in range(16):
            part = parts[j * len(parts) // 16]
            at = (j * 16) % part.shape[0]
            start = pl.multiple_of(block_of(place, orders, j) * 16, 16)
            have = out[pl.ds(start, 16), :].astype(F32)
            out[pl.ds(start, 16), :] = (have + part[at : at + 16, :].astype(F32)).astype(BF16)


def combine(place, own, got, far0, far1):
    return pl.pallas_call(
        combine_kernel,
        out_shape=jax.ShapeDtypeStruct((256, 2048), BF16),
        in_specs=[pl.BlockSpec(memory_space=pltpu.SMEM)]
        + [pl.BlockSpec(memory_space=pltpu.VMEM)] * 4,
        out_specs=pl.BlockSpec(memory_space=pltpu.VMEM),
        compiler_params=pltpu.CompilerParams(vmem_limit_bytes=8 << 20),
        cost_estimate=TINY,
    )(place, own, got, far0, far1)


def partial_product(cot, weight):
    return lax.dot_general(
        cot, weight, (((1,), (1,)), ((), ())), preferred_element_type=F32
    ).astype(BF16)


def weight_kernel(streams, n_grams, place, *refs):
    grams, parts, (out, cot) = refs[:n_grams], refs[n_grams:-2], refs[-2:]

    @pl.when(pl.program_id(0) == 0)
    def _():
        held = [(part, at) for part in parts for at in range(0, part.shape[0], 16)]
        for k, (part, at) in enumerate(held):
            (group, orders), j = streams[k // 16], k % 16
            to = group // 2 * 512 + group % 2 * 16 + block_of(place, orders, j) * 32
            cot[pl.ds(pl.multiple_of(to, 16), 16), :] = part[at : at + 16, :]

    g = jnp.concatenate([part[...] for part in grams], 0)
    for at in range(0, 2048, 512):
        total = lax.dot_general(
            g, cot[:, at : at + 512], (((0,), (0,)), ((), ())), preferred_element_type=F32
        )
        out[:, at : at + 512] = total.astype(BF16)


def weight_product(place, grams, cots, streams, tile=512):
    return pl.pallas_call(
        functools.partial(weight_kernel, streams, len(grams)),
        grid=(2048 // tile,),
        out_shape=jax.ShapeDtypeStruct((2048, 2048), BF16),
        in_specs=[pl.BlockSpec(memory_space=pltpu.SMEM)]
        + [pl.BlockSpec((gram.shape[0], tile), lambda i: (0, i)) for gram in grams]
        + [pl.BlockSpec(cot.shape, lambda i: (0, 0)) for cot in cots],
        out_specs=pl.BlockSpec((tile, 2048), lambda i: (i, 0)),
        scratch_shapes=[pltpu.VMEM((1024, 2048), BF16)],
        compiler_params=pltpu.CompilerParams(vmem_limit_bytes=48 << 20),
        cost_estimate=pl.CostEstimate(
            flops=2 * 1024 * 2048 * 2048, bytes_accessed=16 << 20, transcendentals=0
        ),
    )(place, *grams, *cots)


def group_kernel(place, cot, other, *outs):
    yh, col = place[3], place[4]
    for k, out in enumerate(outs):
        out[yh] = cot[col ^ k]
        out[1 - yh] = other[col ^ k]


def groups(place, cot, other):
    vmem = pl.BlockSpec(memory_space=pltpu.VMEM)
    out = pl.pallas_call(
        group_kernel,
        out_shape=[jax.ShapeDtypeStruct((2, 8, 2048), BF16)] * 4,
        in_specs=[pl.BlockSpec(memory_space=pltpu.SMEM), vmem, vmem],
        out_specs=[vmem] * 4,
        compiler_params=pltpu.CompilerParams(vmem_limit_bytes=2 << 20),
        cost_estimate=pl.CostEstimate(flops=0, bytes_accessed=1 << 20, transcendentals=0),
    )(place, cot.reshape(4, 8, 2048), other.reshape(4, 8, 2048))
    return [part.reshape(16, 2048) for part in out]


def add(*terms):
    total = terms[0].astype(F32)
    for term in terms[1:]:
        total = total + term.astype(F32)
    return total.astype(BF16)


def core_swap(value, size=64):
    return jnp.concatenate(
        [swap(value[i : i + size], core=1) for i in range(0, value.shape[0], size)], 0
    )


def after(value, *others):
    return lax.optimization_barrier((value,) + others)[0]


def gram_part(some, embeds):
    some = some.reshape(some.shape[0], 128, some.shape[-1])
    gram = jnp.einsum("sid,sjd->sij", some, embeds, preferred_element_type=F32).astype(BF16)
    return gram.reshape(gram.shape[0], 16, 2048).transpose(1, 0, 2)


def body(embeds, panel_weight, cotangent):
    local_count, field_count, width = embeds.shape
    row, col = lax.axis_index("row"), lax.axis_index("col")
    x, z, yh = row // 8, (row // 2) % 4, row % 2
    place = jnp.stack([x, z, col % 2, yh, col]).astype(jnp.int32)

    other = swap(cotangent, yh=1)
    near0, near1, far0, far1 = groups(place, cotangent, other)

    split = embeds.reshape(local_count, 16, 2, 8, width)
    gram_sent = gram_part(lax.dynamic_index_in_dim(split, 1 - yh, 2, keepdims=False), embeds)
    gram_kept = gram_part(lax.dynamic_index_in_dim(split, yh, 2, keepdims=False), embeds)
    gram_cross = swap(gram_sent, yh=1, yl=1)
    gram_side = swap(gram_kept, yl=1)
    gram_far_side = swap(gram_cross, yl=1)

    far0 = doubled(far0, FAR, range(2))
    far1 = doubled(far1, FAR_OTHER, range(2))
    far0, gram_cross, gram_side = lax.optimization_barrier((far0, gram_cross, gram_side))
    far0 = doubled(far0, FAR, (2,))
    far1 = doubled(far1, FAR_OTHER, (2,))
    far0_late = step_swap(far0, FAR, 3)
    far1_late = step_swap(far1, FAR_OTHER, 3)
    near = doubled(jnp.stack([near0, near1]), NEAR, range(4))

    both = partial_product(jnp.concatenate([far1, far0], 0), panel_weight)
    far_sum = add(after(both[128:], gram_far_side, far0_late, far1_late), core_swap(both[:128]))
    far_got = swap(far_sum, yl=1)
    both = partial_product(jnp.concatenate([after(far1_late, far_sum), far0_late], 0), panel_weight)
    far_sum_late = add(after(both[128:], far_got), core_swap(both[:128]))
    far_got_late = swap(far_sum_late, yl=1)

    gram_kept = after(gram_kept, far_sum)
    gram = jnp.stack(
        [
            jnp.where(yh == 0, gram_kept, gram_far_side),
            jnp.where(yh == 0, gram_far_side, gram_kept),
            jnp.where(yh == 0, gram_side, gram_cross),
            jnp.where(yh == 0, gram_cross, gram_side),
        ],
        1,
    )
    gram_own = lax.all_to_all(
        gram.reshape(16, 32, 2048), "row", split_axis=0, concat_axis=0, tiled=True,
        axis_index_groups=[list(range(h, 32, 2)) for h in range(2)],
    )
    gram_own = gram_own.reshape(512, 2048)

    near_got = core_swap(partial_product(after(near, far_sum_late)[1], panel_weight))
    kept = partial_product(near[0], panel_weight)
    summed = combine(place, kept, near_got, far_got, far_got_late)
    grad_gram = lax.all_to_all(
        summed.reshape(32, 8, 2048), "row", split_axis=0, concat_axis=0, tiled=True
    )

    ready = after(gram_own, summed)
    gram_core = [swap(ready[i : i + 128], core=1) for i in range(0, 512, 128)]
    cots = (near.reshape(512, 2048), far0, far0_late, far1, far1_late)
    weight_grad = weight_product(
        place, (gram_own, *gram_core), cots, ((0, NEAR), (2, NEAR), (1, FAR), (3, FAR_OTHER))
    )

    grad_gram = after(grad_gram, weight_grad).transpose(1, 0, 2).reshape(local_count, field_count * field_count)
    grad_gram = lax.optimization_barrier(grad_gram)
    grad_gram = grad_gram.reshape(local_count, field_count, field_count)
    embed_grad = jnp.einsum("sij,sjd->sid", grad_gram, embeds, preferred_element_type=F32)
    embed_grad = embed_grad + jnp.einsum(
        "sji,sjd->sid", grad_gram, embeds, preferred_element_type=F32
    )
    return weight_grad, embed_grad.astype(BF16)


def solution(mesh):
    placed = (P(("row", "col"), None, None), P("row", "col"), P("row", "col"))
    return jax.shard_map(
        body,
        mesh=mesh,
        in_specs=placed,
        out_specs=(P("row", "col"), P(("row", "col"), None, None)),
        check_vma=False,
    )
```

```python
import functools

import jax
import jax.numpy as jnp
from jax import lax
from jax.experimental import pallas as pl
from jax.experimental.pallas import tpu as pltpu
from jax.sharding import PartitionSpec as P

AXES = ("row", "col")
MASK = {"a": 1, "b": 3}
BF16 = jnp.bfloat16
F32 = jnp.float32
TINY = pl.CostEstimate(flops=1000, bytes_accessed=1000, transcendentals=0)
FAR = (("xa", "za", "xb", "zb"), ("za", "xa", "zb", "xb"))
FAR_OTHER = FAR[::-1]
NEAR = (("xb", "zb", "xa", "za"), ("zb", "xb", "za", "xa"))
NEAR_OTHER = NEAR[::-1]


def pairs(flips):
    out = []
    for device in range(128):
        place = {
            "core": device & 1,
            "yl": (device >> 1) & 1,
            "yh": (device >> 2) & 1,
            "z": (device >> 3) & 3,
            "x": (device >> 5) & 3,
        }
        for axis, mask in flips[device & 1].items():
            place[axis] ^= mask
        other = (place["x"] * 4 + place["z"]) * 2 + place["yh"]
        out.append((device, (other * 2 + place["yl"]) * 2 + place["core"]))
    return out


def swap(value, **flips):
    return lax.ppermute(value, AXES, pairs((flips, flips)))


def step_swap(value, orders, t):
    flips = [{order[t][0]: MASK[order[t][1]]} for order in orders]
    return lax.ppermute(value, AXES, pairs(flips))


def doubled(value, orders, steps):
    for t in steps:
        value = jnp.concatenate([value, step_swap(value, orders, t)], -2)
    return value


def masks(order, j):
    mx = mz = 0
    for t, step in enumerate(order):
        if (j >> t) & 1:
            if step[0] == "x":
                mx ^= MASK[step[1]]
            else:
                mz ^= MASK[step[1]]
    return mx, mz


def block_of(place, orders, j):
    x, z, core = place[0], place[1], place[2]
    first, second = masks(orders[0], j), masks(orders[1], j)
    if first == second:
        return (x ^ first[0]) * 4 + (z ^ first[1])
    mx = jnp.where(core == 0, first[0], second[0])
    mz = jnp.where(core == 0, first[1], second[1])
    return (x ^ mx) * 4 + (z ^ mz)


def combine_kernel(place, own, got, far0, far1, out):
    for j in range(16):
        start = pl.multiple_of(block_of(place, NEAR, j) * 16, 16)
        out[pl.ds(start, 16), :] = own[j * 16 : j * 16 + 16, :]
    for orders, parts in ((NEAR_OTHER, (got,)), (FAR, (far0, far1))):
        for j in range(16):
            part = parts[j * len(parts) // 16]
            at = (j * 16) % part.shape[0]
            start = pl.multiple_of(block_of(place, orders, j) * 16, 16)
            have = out[pl.ds(start, 16), :].astype(F32)
            out[pl.ds(start, 16), :] = (have + part[at : at + 16, :].astype(F32)).astype(BF16)


def combine(place, own, got, far0, far1):
    return pl.pallas_call(
        combine_kernel,
        out_shape=jax.ShapeDtypeStruct((256, 2048), BF16),
        in_specs=[pl.BlockSpec(memory_space=pltpu.SMEM)]
        + [pl.BlockSpec(memory_space=pltpu.VMEM)] * 4,
        out_specs=pl.BlockSpec(memory_space=pltpu.VMEM),
        compiler_params=pltpu.CompilerParams(vmem_limit_bytes=8 << 20),
        cost_estimate=TINY,
    )(place, own, got, far0, far1)


def partial_product(cot, weight):
    return lax.dot_general(
        cot, weight, (((1,), (1,)), ((), ())), preferred_element_type=F32
    ).astype(BF16)


def assemble_kernel(streams, place, *refs):
    parts, out = refs[:-1], refs[-1]
    held = [(part, at) for part in parts for at in range(0, part.shape[0], 16)]
    for k, (part, at) in enumerate(held):
        (group, orders), j = streams[k // 16], k % 16
        to = group // 2 * 512 + group % 2 * 16 + block_of(place, orders, j) * 32
        out[pl.ds(pl.multiple_of(to, 16), 16), :] = part[at : at + 16, :]


def assemble(place, cots, streams):
    return pl.pallas_call(
        functools.partial(assemble_kernel, streams),
        grid=(1,),
        out_shape=jax.ShapeDtypeStruct((1024, 2048), BF16),
        in_specs=[pl.BlockSpec(memory_space=pltpu.SMEM)]
        + [pl.BlockSpec(cot.shape, lambda i: (0, 0)) for cot in cots],
        out_specs=pl.BlockSpec((1024, 2048), lambda i: (0, 0)),
        compiler_params=pltpu.CompilerParams(vmem_limit_bytes=32 << 20),
        cost_estimate=TINY,
    )(place, *cots)


def weight_kernel(*refs):
    grams, (cot, out) = refs[:-2], refs[-2:]
    g = jnp.concatenate([part[...] for part in grams], 0)
    for at in range(0, 2048, 512):
        total = lax.dot_general(
            g, cot[:, at : at + 512], (((0,), (0,)), ((), ())), preferred_element_type=F32
        )
        out[:, at : at + 512] = total.astype(BF16)


def weight_product(grams, cot, tile=512):
    return pl.pallas_call(
        weight_kernel,
        grid=(2048 // tile,),
        out_shape=jax.ShapeDtypeStruct((2048, 2048), BF16),
        in_specs=[pl.BlockSpec((gram.shape[0], tile), lambda i: (0, i)) for gram in grams]
        + [pl.BlockSpec((1024, 2048), lambda i: (0, 0))],
        out_specs=pl.BlockSpec((tile, 2048), lambda i: (i, 0)),
        compiler_params=pltpu.CompilerParams(vmem_limit_bytes=48 << 20),
        cost_estimate=TINY,
    )(*grams, cot)


def group_kernel(place, cot, other, *outs):
    yh, col = place[3], place[4]
    for k, out in enumerate(outs):
        out[yh] = cot[col ^ k]
        out[1 - yh] = other[col ^ k]


def groups(place, cot, other):
    vmem = pl.BlockSpec(memory_space=pltpu.VMEM)
    out = pl.pallas_call(
        group_kernel,
        out_shape=[jax.ShapeDtypeStruct((2, 8, 2048), BF16)] * 4,
        in_specs=[pl.BlockSpec(memory_space=pltpu.SMEM), vmem, vmem],
        out_specs=[vmem] * 4,
        compiler_params=pltpu.CompilerParams(vmem_limit_bytes=2 << 20),
        cost_estimate=pl.CostEstimate(flops=0, bytes_accessed=1 << 20, transcendentals=0),
    )(place, cot.reshape(4, 8, 2048), other.reshape(4, 8, 2048))
    return [part.reshape(16, 2048) for part in out]


def add(*terms):
    total = terms[0].astype(F32)
    for term in terms[1:]:
        total = total + term.astype(F32)
    return total.astype(BF16)


def core_swap(value, size=64):
    return jnp.concatenate(
        [swap(value[i : i + size], core=1) for i in range(0, value.shape[0], size)], 0
    )


def after(value, *others):
    return lax.optimization_barrier((value,) + others)[0]


def gram_part(some, embeds):
    some = some.reshape(some.shape[0], 128, some.shape[-1])
    gram = jnp.einsum("sid,sjd->sij", some, embeds, preferred_element_type=F32).astype(BF16)
    return gram.reshape(gram.shape[0], 16, 2048).transpose(1, 0, 2)


def body(embeds, panel_weight, cotangent):
    local_count, field_count, width = embeds.shape
    row, col = lax.axis_index("row"), lax.axis_index("col")
    x, z, yh = row // 8, (row // 2) % 4, row % 2
    place = jnp.stack([x, z, col % 2, yh, col]).astype(jnp.int32)

    other = swap(cotangent, yh=1)
    near0, near1, far0, far1 = groups(place, cotangent, other)

    split = embeds.reshape(local_count, 16, 2, 8, width)
    gram_sent = gram_part(lax.dynamic_index_in_dim(split, 1 - yh, 2, keepdims=False), embeds)
    gram_kept = gram_part(lax.dynamic_index_in_dim(split, yh, 2, keepdims=False), embeds)
    gram_cross = swap(gram_sent, yh=1, yl=1)
    gram_side = swap(gram_kept, yl=1)
    gram_far_side = swap(gram_cross, yl=1)

    far0 = doubled(far0, FAR, range(2))
    far1 = doubled(far1, FAR_OTHER, range(2))
    far0, gram_cross, gram_side = lax.optimization_barrier((far0, gram_cross, gram_side))
    far0 = doubled(far0, FAR, (2,))
    far1 = doubled(far1, FAR_OTHER, (2,))
    far0_late = step_swap(far0, FAR, 3)
    far1_late = step_swap(far1, FAR_OTHER, 3)
    near = doubled(jnp.stack([near0, near1]), NEAR, range(4))

    both = partial_product(jnp.concatenate([far1, far0], 0), panel_weight)
    far_sum = add(after(both[128:], gram_far_side, far0_late, far1_late), core_swap(both[:128]))
    far_got = swap(far_sum, yl=1)
    both = partial_product(jnp.concatenate([after(far1_late, far_sum), far0_late], 0), panel_weight)
    far_sum_late = add(after(both[128:], far_got), core_swap(both[:128]))
    far_got_late = swap(far_sum_late, yl=1)

    gram_kept = after(gram_kept, far_sum)
    gram = jnp.stack(
        [
            jnp.where(yh == 0, gram_kept, gram_far_side),
            jnp.where(yh == 0, gram_far_side, gram_kept),
            jnp.where(yh == 0, gram_side, gram_cross),
            jnp.where(yh == 0, gram_cross, gram_side),
        ],
        1,
    )
    gram_own = lax.all_to_all(
        gram.reshape(16, 32, 2048), "row", split_axis=0, concat_axis=0, tiled=True,
        axis_index_groups=[list(range(h, 32, 2)) for h in range(2)],
    )
    gram_own = gram_own.reshape(512, 2048)

    near_got = core_swap(partial_product(after(near, far_sum_late)[1], panel_weight))
    kept = partial_product(near[0], panel_weight)
    cots = (near.reshape(512, 2048), far0, far0_late, far1, far1_late)
    cot = assemble(after(place, kept), cots, ((0, NEAR), (2, NEAR), (1, FAR), (3, FAR_OTHER)))
    summed = combine(place, kept, near_got, far_got, far_got_late)
    grad_gram = lax.all_to_all(
        summed.reshape(32, 8, 2048), "row", split_axis=0, concat_axis=0, tiled=True
    )

    ready = after(gram_own, summed, cot)
    gram_core = [swap(ready[i : i + 128], core=1) for i in range(0, 512, 128)]
    weight_grad = weight_product((gram_own, *gram_core), cot)

    grad_gram = after(grad_gram, weight_grad).transpose(1, 0, 2).reshape(local_count, field_count * field_count)
    grad_gram = lax.optimization_barrier(grad_gram)
    grad_gram = grad_gram.reshape(local_count, field_count, field_count)
    embed_grad = jnp.einsum("sij,sjd->sid", grad_gram, embeds, preferred_element_type=F32)
    embed_grad = embed_grad + jnp.einsum(
        "sji,sjd->sid", grad_gram, embeds, preferred_element_type=F32
    )
    return weight_grad, embed_grad.astype(BF16)


def solution(mesh):
    placed = (P(("row", "col"), None, None), P("row", "col"), P("row", "col"))
    return jax.shard_map(
        body,
        mesh=mesh,
        in_specs=placed,
        out_specs=(P("row", "col"), P(("row", "col"), None, None)),
        check_vma=False,
    )
```

```python
import functools

import jax
import jax.numpy as jnp
from jax import lax
from jax.experimental import pallas as pl
from jax.experimental.pallas import tpu as pltpu
from jax.sharding import PartitionSpec as P

AXES = ("row", "col")
MASK = {"a": 1, "b": 3}
BF16 = jnp.bfloat16
F32 = jnp.float32
TINY = pl.CostEstimate(flops=1000, bytes_accessed=1000, transcendentals=0)
FAR = (("xa", "za", "xb", "zb"), ("za", "xa", "zb", "xb"))
FAR_OTHER = FAR[::-1]
NEAR = (("xb", "zb", "xa", "za"), ("zb", "xb", "za", "xa"))
NEAR_OTHER = NEAR[::-1]


def pairs(flips):
    out = []
    for device in range(128):
        place = {
            "core": device & 1,
            "yl": (device >> 1) & 1,
            "yh": (device >> 2) & 1,
            "z": (device >> 3) & 3,
            "x": (device >> 5) & 3,
        }
        for axis, mask in flips[device & 1].items():
            place[axis] ^= mask
        other = (place["x"] * 4 + place["z"]) * 2 + place["yh"]
        out.append((device, (other * 2 + place["yl"]) * 2 + place["core"]))
    return out


def swap(value, **flips):
    return lax.ppermute(value, AXES, pairs((flips, flips)))


def step_swap(value, orders, t):
    flips = [{order[t][0]: MASK[order[t][1]]} for order in orders]
    return lax.ppermute(value, AXES, pairs(flips))


def doubled(value, orders, steps):
    for t in steps:
        value = jnp.concatenate([value, step_swap(value, orders, t)], -2)
    return value


def masks(order, j):
    mx = mz = 0
    for t, step in enumerate(order):
        if (j >> t) & 1:
            if step[0] == "x":
                mx ^= MASK[step[1]]
            else:
                mz ^= MASK[step[1]]
    return mx, mz


def block_of(place, orders, j):
    x, z, core = place[0], place[1], place[2]
    first, second = masks(orders[0], j), masks(orders[1], j)
    if first == second:
        return (x ^ first[0]) * 4 + (z ^ first[1])
    mx = jnp.where(core == 0, first[0], second[0])
    mz = jnp.where(core == 0, first[1], second[1])
    return (x ^ mx) * 4 + (z ^ mz)


def combine_kernel(place, own, got, far0, far1, out):
    for j in range(16):
        start = pl.multiple_of(block_of(place, NEAR, j) * 16, 16)
        out[pl.ds(start, 16), :] = own[j * 16 : j * 16 + 16, :]
    for orders, parts in ((NEAR_OTHER, (got,)), (FAR, (far0, far1))):
        for j in range(16):
            part = parts[j * len(parts) // 16]
            at = (j * 16) % part.shape[0]
            start = pl.multiple_of(block_of(place, orders, j) * 16, 16)
            have = out[pl.ds(start, 16), :].astype(F32)
            out[pl.ds(start, 16), :] = (have + part[at : at + 16, :].astype(F32)).astype(BF16)


def combine(place, own, got, far0, far1):
    return pl.pallas_call(
        combine_kernel,
        out_shape=jax.ShapeDtypeStruct((256, 2048), BF16),
        in_specs=[pl.BlockSpec(memory_space=pltpu.SMEM)]
        + [pl.BlockSpec(memory_space=pltpu.VMEM)] * 4,
        out_specs=pl.BlockSpec(memory_space=pltpu.VMEM),
        compiler_params=pltpu.CompilerParams(vmem_limit_bytes=8 << 20),
        cost_estimate=TINY,
    )(place, own, got, far0, far1)


def partial_product(cot, weight):
    return lax.dot_general(
        cot, weight, (((1,), (1,)), ((), ())), preferred_element_type=F32
    ).astype(BF16)


def assemble_kernel(streams, place, *refs):
    parts, out = refs[:-1], refs[-1]
    held = [(part, at) for part in parts for at in range(0, part.shape[0], 16)]
    for k, (part, at) in enumerate(held):
        (group, orders), j = streams[k // 16], k % 16
        to = group // 2 * 512 + group % 2 * 16 + block_of(place, orders, j) * 32
        out[pl.ds(pl.multiple_of(to, 16), 16), :] = part[at : at + 16, :]


def assemble(place, cots, streams):
    return pl.pallas_call(
        functools.partial(assemble_kernel, streams),
        grid=(1,),
        out_shape=jax.ShapeDtypeStruct((1024, 2048), BF16),
        in_specs=[pl.BlockSpec(memory_space=pltpu.SMEM)]
        + [pl.BlockSpec(cot.shape, lambda i: (0, 0)) for cot in cots],
        out_specs=pl.BlockSpec((1024, 2048), lambda i: (0, 0)),
        compiler_params=pltpu.CompilerParams(vmem_limit_bytes=32 << 20),
        cost_estimate=TINY,
    )(place, *cots)


def weight_kernel(*refs):
    grams, (cot, out) = refs[:-2], refs[-2:]
    g = jnp.concatenate([part[...] for part in grams], 0)
    for at in range(0, out.shape[1], 512):
        total = lax.dot_general(
            g, cot[:, at : at + 512], (((0,), (0,)), ((), ())), preferred_element_type=F32
        )
        out[:, at : at + 512] = total.astype(BF16)


def weight_product(grams, cot, rows=2048, cols=512):
    return pl.pallas_call(
        weight_kernel,
        grid=(2048 // cols, 2048 // rows),
        out_shape=jax.ShapeDtypeStruct((2048, 2048), BF16),
        in_specs=[pl.BlockSpec((gram.shape[0], rows), lambda j, i: (0, i)) for gram in grams]
        + [pl.BlockSpec((1024, cols), lambda j, i: (0, j))],
        out_specs=pl.BlockSpec((rows, cols), lambda j, i: (i, j)),
        compiler_params=pltpu.CompilerParams(vmem_limit_bytes=48 << 20),
        cost_estimate=TINY,
    )(*grams, cot)


def group_kernel(place, cot, other, *outs):
    yh, col = place[3], place[4]
    for k, out in enumerate(outs):
        out[yh] = cot[col ^ k]
        out[1 - yh] = other[col ^ k]


def groups(place, cot, other):
    vmem = pl.BlockSpec(memory_space=pltpu.VMEM)
    out = pl.pallas_call(
        group_kernel,
        out_shape=[jax.ShapeDtypeStruct((2, 8, 2048), BF16)] * 4,
        in_specs=[pl.BlockSpec(memory_space=pltpu.SMEM), vmem, vmem],
        out_specs=[vmem] * 4,
        compiler_params=pltpu.CompilerParams(vmem_limit_bytes=2 << 20),
        cost_estimate=pl.CostEstimate(flops=0, bytes_accessed=1 << 20, transcendentals=0),
    )(place, cot.reshape(4, 8, 2048), other.reshape(4, 8, 2048))
    return [part.reshape(16, 2048) for part in out]


def add(*terms):
    total = terms[0].astype(F32)
    for term in terms[1:]:
        total = total + term.astype(F32)
    return total.astype(BF16)


def core_swap(value, size=64):
    return jnp.concatenate(
        [swap(value[i : i + size], core=1) for i in range(0, value.shape[0], size)], 0
    )


def after(value, *others):
    return lax.optimization_barrier((value,) + others)[0]


def gram_part(some, embeds):
    some = some.reshape(some.shape[0], 128, some.shape[-1])
    gram = jnp.einsum("sid,sjd->sij", some, embeds, preferred_element_type=F32).astype(BF16)
    return gram.reshape(gram.shape[0], 16, 2048).transpose(1, 0, 2)


def body(embeds, panel_weight, cotangent):
    local_count, field_count, width = embeds.shape
    row, col = lax.axis_index("row"), lax.axis_index("col")
    x, z, yh = row // 8, (row // 2) % 4, row % 2
    place = jnp.stack([x, z, col % 2, yh, col]).astype(jnp.int32)

    other = swap(cotangent, yh=1)
    near0, near1, far0, far1 = groups(place, cotangent, other)

    split = embeds.reshape(local_count, 16, 2, 8, width)
    gram_sent = gram_part(lax.dynamic_index_in_dim(split, 1 - yh, 2, keepdims=False), embeds)
    gram_kept = gram_part(lax.dynamic_index_in_dim(split, yh, 2, keepdims=False), embeds)
    gram_cross = swap(gram_sent, yh=1, yl=1)
    gram_side = swap(gram_kept, yl=1)
    gram_far_side = swap(gram_cross, yl=1)

    far0 = doubled(far0, FAR, range(2))
    far1 = doubled(far1, FAR_OTHER, range(2))
    far0, gram_cross, gram_side = lax.optimization_barrier((far0, gram_cross, gram_side))
    far0 = doubled(far0, FAR, (2,))
    far1 = doubled(far1, FAR_OTHER, (2,))
    far0_late = step_swap(far0, FAR, 3)
    far1_late = step_swap(far1, FAR_OTHER, 3)
    near = doubled(jnp.stack([near0, near1]), NEAR, range(4))

    both = partial_product(jnp.concatenate([far1, far0], 0), panel_weight)
    far_sum = add(after(both, gram_far_side, far0_late, far1_late)[128:], core_swap(both[:128]))
    far_got = swap(far_sum, yl=1)
    both = partial_product(jnp.concatenate([after(far1_late, far_sum), far0_late], 0), panel_weight)
    far_sum_late = add(after(both, far_got)[128:], core_swap(both[:128]))
    far_got_late = swap(far_sum_late, yl=1)

    gram_kept = after(gram_kept, far_sum)
    gram = jnp.stack(
        [
            jnp.where(yh == 0, gram_kept, gram_far_side),
            jnp.where(yh == 0, gram_far_side, gram_kept),
            jnp.where(yh == 0, gram_side, gram_cross),
            jnp.where(yh == 0, gram_cross, gram_side),
        ],
        1,
    )
    gram_own = lax.all_to_all(
        gram.reshape(16, 32, 2048), "row", split_axis=0, concat_axis=0, tiled=True,
        axis_index_groups=[list(range(h, 32, 2)) for h in range(2)],
    )
    gram_own = gram_own.reshape(512, 2048)

    near_got = core_swap(partial_product(after(near, far_sum_late)[1], panel_weight))
    kept = partial_product(near[0], panel_weight)
    cots = (near.reshape(512, 2048), far0, far0_late, far1, far1_late)
    cot = assemble(after(place, kept), cots, ((0, NEAR), (2, NEAR), (1, FAR), (3, FAR_OTHER)))
    summed = combine(place, kept, near_got, far_got, far_got_late)
    grad_gram = lax.all_to_all(
        summed.reshape(32, 8, 2048), "row", split_axis=0, concat_axis=0, tiled=True
    )

    ready = after(gram_own, summed, cot)
    gram_core = [swap(ready[i : i + 128], core=1) for i in range(0, 512, 128)]
    weight_grad = weight_product((gram_own, *gram_core), cot)

    grad_gram = after(grad_gram, weight_grad).transpose(1, 0, 2).reshape(local_count, field_count * field_count)
    grad_gram = lax.optimization_barrier(grad_gram)
    grad_gram = grad_gram.reshape(local_count, field_count, field_count)
    embed_grad = jnp.einsum("sij,sjd->sid", grad_gram, embeds, preferred_element_type=F32)
    embed_grad = embed_grad + jnp.einsum(
        "sji,sjd->sid", grad_gram, embeds, preferred_element_type=F32
    )
    return weight_grad, embed_grad.astype(BF16)


def solution(mesh):
    placed = (P(("row", "col"), None, None), P("row", "col"), P("row", "col"))
    return jax.shard_map(
        body,
        mesh=mesh,
        in_specs=placed,
        out_specs=(P("row", "col"), P(("row", "col"), None, None)),
        check_vma=False,
    )
```

```python
import functools

import jax
import jax.numpy as jnp
from jax import lax
from jax.experimental import pallas as pl
from jax.experimental.pallas import tpu as pltpu
from jax.sharding import PartitionSpec as P

AXES = ("row", "col")
MASK = {"a": 1, "b": 3}
BF16 = jnp.bfloat16
F32 = jnp.float32
TINY = pl.CostEstimate(flops=1000, bytes_accessed=1000, transcendentals=0)
FAR = (("xa", "za", "xb", "zb"), ("za", "xa", "zb", "xb"))
FAR_OTHER = FAR[::-1]
NEAR = (("xb", "zb", "xa", "za"), ("zb", "xb", "za", "xa"))
NEAR_OTHER = NEAR[::-1]


def pairs(flips):
    out = []
    for device in range(128):
        place = {
            "core": device & 1,
            "yl": (device >> 1) & 1,
            "yh": (device >> 2) & 1,
            "z": (device >> 3) & 3,
            "x": (device >> 5) & 3,
        }
        for axis, mask in flips[device & 1].items():
            place[axis] ^= mask
        other = (place["x"] * 4 + place["z"]) * 2 + place["yh"]
        out.append((device, (other * 2 + place["yl"]) * 2 + place["core"]))
    return out


def swap(value, **flips):
    return lax.ppermute(value, AXES, pairs((flips, flips)))


def step_swap(value, orders, t):
    flips = [{order[t][0]: MASK[order[t][1]]} for order in orders]
    return lax.ppermute(value, AXES, pairs(flips))


def doubled(value, orders, steps):
    for t in steps:
        value = jnp.concatenate([value, step_swap(value, orders, t)], -2)
    return value


def masks(order, j):
    mx = mz = 0
    for t, step in enumerate(order):
        if (j >> t) & 1:
            if step[0] == "x":
                mx ^= MASK[step[1]]
            else:
                mz ^= MASK[step[1]]
    return mx, mz


def block_of(place, orders, j):
    x, z, core = place[0], place[1], place[2]
    first, second = masks(orders[0], j), masks(orders[1], j)
    if first == second:
        return (x ^ first[0]) * 4 + (z ^ first[1])
    mx = jnp.where(core == 0, first[0], second[0])
    mz = jnp.where(core == 0, first[1], second[1])
    return (x ^ mx) * 4 + (z ^ mz)


def combine_kernel(place, own, got, far0, far1, out):
    for j in range(16):
        start = pl.multiple_of(block_of(place, NEAR, j) * 16, 16)
        out[pl.ds(start, 16), :] = own[j * 16 : j * 16 + 16, :]
    for orders, parts in ((NEAR_OTHER, (got,)), (FAR, (far0, far1))):
        for j in range(16):
            part = parts[j * len(parts) // 16]
            at = (j * 16) % part.shape[0]
            start = pl.multiple_of(block_of(place, orders, j) * 16, 16)
            have = out[pl.ds(start, 16), :].astype(F32)
            out[pl.ds(start, 16), :] = (have + part[at : at + 16, :].astype(F32)).astype(BF16)


def combine(place, own, got, far0, far1):
    return pl.pallas_call(
        combine_kernel,
        out_shape=jax.ShapeDtypeStruct((256, 2048), BF16),
        in_specs=[pl.BlockSpec(memory_space=pltpu.SMEM)]
        + [pl.BlockSpec(memory_space=pltpu.VMEM)] * 4,
        out_specs=pl.BlockSpec(memory_space=pltpu.VMEM),
        compiler_params=pltpu.CompilerParams(vmem_limit_bytes=8 << 20),
        cost_estimate=TINY,
    )(place, own, got, far0, far1)


def partial_product(cot, weight):
    return lax.dot_general(
        cot, weight, (((1,), (1,)), ((), ())), preferred_element_type=F32
    ).astype(BF16)


def assemble_kernel(streams, place, *refs):
    parts, out = refs[:-1], refs[-1]
    held = [(part, at) for part in parts for at in range(0, part.shape[0], 16)]
    for k, (part, at) in enumerate(held):
        (group, orders), j = streams[k // 16], k % 16
        to = group // 2 * 512 + group % 2 * 16 + block_of(place, orders, j) * 32
        out[pl.ds(pl.multiple_of(to, 16), 16), :] = part[at : at + 16, :]


def assemble(place, cots, streams):
    return pl.pallas_call(
        functools.partial(assemble_kernel, streams),
        grid=(1,),
        out_shape=jax.ShapeDtypeStruct((1024, 2048), BF16),
        in_specs=[pl.BlockSpec(memory_space=pltpu.SMEM)]
        + [pl.BlockSpec(cot.shape, lambda i: (0, 0)) for cot in cots],
        out_specs=pl.BlockSpec((1024, 2048), lambda i: (0, 0)),
        compiler_params=pltpu.CompilerParams(vmem_limit_bytes=32 << 20),
        cost_estimate=TINY,
    )(place, *cots)


def weight_kernel(*refs):
    grams, (cot, out) = refs[:-2], refs[-2:]
    cols = out.shape[1]
    at = pl.multiple_of(pl.program_id(0) * cols, cols)
    g = jnp.concatenate([part[...] for part in grams], 0)
    total = lax.dot_general(
        g, cot[:, pl.ds(at, cols)], (((0,), (0,)), ((), ())), preferred_element_type=F32
    )
    out[...] = total.astype(BF16)


def weight_product(grams, cot, cols=512):
    return pl.pallas_call(
        weight_kernel,
        grid=(2048 // cols,),
        out_shape=jax.ShapeDtypeStruct((2048, 2048), BF16),
        in_specs=[pl.BlockSpec(memory_space=pltpu.VMEM)] * (len(grams) + 1),
        out_specs=pl.BlockSpec((2048, cols), lambda j: (0, j)),
        compiler_params=pltpu.CompilerParams(vmem_limit_bytes=28 << 20),
        cost_estimate=TINY,
    )(*grams, cot)


def group_kernel(place, cot, other, *outs):
    yh, col = place[3], place[4]
    for k, out in enumerate(outs):
        out[yh] = cot[col ^ k]
        out[1 - yh] = other[col ^ k]


def groups(place, cot, other):
    vmem = pl.BlockSpec(memory_space=pltpu.VMEM)
    out = pl.pallas_call(
        group_kernel,
        out_shape=[jax.ShapeDtypeStruct((2, 8, 2048), BF16)] * 4,
        in_specs=[pl.BlockSpec(memory_space=pltpu.SMEM), vmem, vmem],
        out_specs=[vmem] * 4,
        compiler_params=pltpu.CompilerParams(vmem_limit_bytes=2 << 20),
        cost_estimate=pl.CostEstimate(flops=0, bytes_accessed=1 << 20, transcendentals=0),
    )(place, cot.reshape(4, 8, 2048), other.reshape(4, 8, 2048))
    return [part.reshape(16, 2048) for part in out]


def add(*terms):
    total = terms[0].astype(F32)
    for term in terms[1:]:
        total = total + term.astype(F32)
    return total.astype(BF16)


def core_swap(value, size=64):
    return jnp.concatenate(
        [swap(value[i : i + size], core=1) for i in range(0, value.shape[0], size)], 0
    )


def after(value, *others):
    return lax.optimization_barrier((value,) + others)[0]


def gram_part(some, embeds):
    some = some.reshape(some.shape[0], 128, some.shape[-1])
    gram = jnp.einsum("sid,sjd->sij", some, embeds, preferred_element_type=F32).astype(BF16)
    return gram.reshape(gram.shape[0], 16, 2048).transpose(1, 0, 2)


def body(embeds, panel_weight, cotangent):
    local_count, field_count, width = embeds.shape
    row, col = lax.axis_index("row"), lax.axis_index("col")
    x, z, yh = row // 8, (row // 2) % 4, row % 2
    place = jnp.stack([x, z, col % 2, yh, col]).astype(jnp.int32)

    other = swap(cotangent, yh=1)
    near0, near1, far0, far1 = groups(place, cotangent, other)

    split = embeds.reshape(local_count, 16, 2, 8, width)
    gram_sent = gram_part(lax.dynamic_index_in_dim(split, 1 - yh, 2, keepdims=False), embeds)
    gram_kept = gram_part(lax.dynamic_index_in_dim(split, yh, 2, keepdims=False), embeds)
    gram_cross = swap(gram_sent, yh=1, yl=1)
    gram_side = swap(gram_kept, yl=1)
    gram_far_side = swap(gram_cross, yl=1)

    far0 = doubled(far0, FAR, range(2))
    far1 = doubled(far1, FAR_OTHER, range(2))
    far0, gram_cross, gram_side = lax.optimization_barrier((far0, gram_cross, gram_side))
    far0 = doubled(far0, FAR, (2,))
    far1 = doubled(far1, FAR_OTHER, (2,))
    far0_late = step_swap(far0, FAR, 3)
    far1_late = step_swap(far1, FAR_OTHER, 3)
    near = doubled(jnp.stack([near0, near1]), NEAR, range(4))

    both = partial_product(jnp.concatenate([far1, far0], 0), panel_weight)
    far_sum = add(after(both, gram_far_side, far0_late, far1_late)[128:], core_swap(both[:128]))
    far_got = swap(far_sum, yl=1)
    both = partial_product(jnp.concatenate([after(far1_late, far_sum), far0_late], 0), panel_weight)
    far_sum_late = add(after(both, far_got)[128:], core_swap(both[:128]))
    far_got_late = swap(far_sum_late, yl=1)

    gram_kept = after(gram_kept, far_sum)
    gram = jnp.stack(
        [
            jnp.where(yh == 0, gram_kept, gram_far_side),
            jnp.where(yh == 0, gram_far_side, gram_kept),
            jnp.where(yh == 0, gram_side, gram_cross),
            jnp.where(yh == 0, gram_cross, gram_side),
        ],
        1,
    )
    gram_own = lax.all_to_all(
        gram.reshape(16, 32, 2048), "row", split_axis=0, concat_axis=0, tiled=True,
        axis_index_groups=[list(range(h, 32, 2)) for h in range(2)],
    )
    gram_own = gram_own.reshape(512, 2048)

    near_got = core_swap(partial_product(after(near, far_sum_late)[1], panel_weight))
    kept = partial_product(near[0], panel_weight)
    cots = (near.reshape(512, 2048), far0, far0_late, far1, far1_late)
    cot = assemble(after(place, kept), cots, ((0, NEAR), (2, NEAR), (1, FAR), (3, FAR_OTHER)))
    summed = combine(place, kept, near_got, far_got, far_got_late)
    grad_gram = lax.all_to_all(
        summed.reshape(32, 8, 2048), "row", split_axis=0, concat_axis=0, tiled=True
    )

    ready = after(gram_own, summed, cot)
    gram_core = [swap(ready[i : i + 128], core=1) for i in range(0, 512, 128)]
    weight_grad = weight_product((gram_own, *gram_core), cot)

    grad_gram = after(grad_gram, weight_grad).transpose(1, 0, 2).reshape(local_count, field_count * field_count)
    grad_gram = lax.optimization_barrier(grad_gram)
    grad_gram = grad_gram.reshape(local_count, field_count, field_count)
    embed_grad = jnp.einsum("sij,sjd->sid", grad_gram, embeds, preferred_element_type=F32)
    embed_grad = embed_grad + jnp.einsum(
        "sji,sjd->sid", grad_gram, embeds, preferred_element_type=F32
    )
    return weight_grad, embed_grad.astype(BF16)


def solution(mesh):
    placed = (P(("row", "col"), None, None), P("row", "col"), P("row", "col"))
    return jax.shard_map(
        body,
        mesh=mesh,
        in_specs=placed,
        out_specs=(P("row", "col"), P(("row", "col"), None, None)),
        check_vma=False,
    )
```
